256 devices in a mesh: row: 8 (over x, core), col: 32 (over z, y).
Axes of the slice: x: 4, y: 4, z: 8, core: 2. Of those that a mesh axis runs over, the one named last changes fastest.
Arguments:
- acts: bfloat16 [2048, 16384], P('row', 'col'), may hold values from -8 to 8
- sample_idx: int32 [8, 96], P('row'), may hold values from 0 to 255
- sample_count: int32 [8], replicated, may hold values from 1 to 96, 256 in all
- codes: bfloat16 [16384, 16384], P('row', 'col'), may hold values from -127 to 127, as said below
- scales: float32 [256, 16384], P('row', 'col'), may hold values from 4e-05 to 0.00016
- grad: bfloat16 [16384, 8192], P('row', 'col'), may hold values from -6 to 6
Outputs:
- new_ema: bfloat16 [16384, 16384], P('row', 'col')
- factor_step: float32 [16384, 16384], P('row', 'col')
- solved: float32 [16384, 8192], P('row', 'col')
The draws below stay inside these ranges and needn't reach their ends.
Inputs may be any that keep to these rules, and one draw needn't show every extreme that they name: `sample_count`: the counts sum to 256; the largest is 96. `sample_idx`: entries k at or past sample_count[g] of row g are unused. `codes`: whole numbers.
All inputs are finite; a program needn't handle non-finite values.
Results may differ from the reference program's by a relative error of at most 0.0056.
Values may be sent and summed in bfloat16 or wider, within the bound.
No kernel may reach another device: no remote copies, remote signals or barrier semaphores. Data moves between devices by JAX's collectives and lax.ppermute only.
A program may use at most 64 MiB of HBM per device.

```python
import math
import jax
import jax.numpy as jnp
import numpy as np
from jax import lax

F = 16384
M = 8192
P_SIZE = 256
QB = 64
LOC = 256
CAP = 96
S = 256
TOKENS = 2048
N_ROW = 8


def draw_codes(key, part):
    values = jax.random.randint(key, (F, F), -127, 128)
    values = values.at[0, 0].set(127).at[1, 0].set(-127)
    return values.astype(jnp.float32).astype(jnp.bfloat16)


def place_ends(result, stream_key, smallest, high):
    index_at = [jax.random.randint(jax.random.fold_in(stream_key, axis), (), 0, length) for axis, length in enumerate(result.shape)]
    widest = result.shape.index(max(result.shape))
    beside = index_at[:widest] + [(index_at[widest] + 1) % result.shape[widest]] + index_at[widest + 1:]
    return result.at[tuple(index_at)].set(smallest).at[tuple(beside)].set(high)


def shard_levels(rng, shape, cuts, smallest, top_value):
    def one(position, blocks):
        steps = jax.random.uniform(jax.random.fold_in(jax.random.fold_in(rng, 6), position), (blocks,), jnp.float32, smallest / len(cuts), top_value / len(cuts))
        return jnp.repeat(jnp.exp(steps), shape[position] // blocks).reshape((-1,) + (1,) * (len(shape) - position - 1))

    gain = one(*cuts[0])
    for cut in cuts[1:]:
        gain = gain * one(*cut)
    return gain


def split_up(amount, total, bound, skew):
    weights = [(1 << 20) // math.isqrt(grade ** skew) + 1 for grade in range(2, amount + 1)]
    surplus, holding = total - bound - (amount - 1), [1] * (amount - 1)
    while surplus > 0:
        movable = [i for i in range(amount - 1) if holding[i] < bound]
        whole, remaining = sum([weights[i] for i in movable]), surplus
        for i in movable:
            extra = min(bound - holding[i], max(1, remaining * weights[i] // whole), surplus)
            holding[i] = holding[i] + extra
            surplus = surplus - extra
    return np.array([bound] + holding)


def uneven_parts(rng, amount, total, most, lean):
    if amount == 2:
        one = jax.random.randint(rng, (), max(1, total - most), min(most, total - 1) + 1)
        return jnp.stack([one, total - one])
    sizes = jnp.asarray(split_up(amount, total, most, lean), jnp.int32)
    couples = (amount - 1) // 2
    donor, sink = sizes[1:1 + 2 * couples:2], sizes[2:2 + 2 * couples:2]
    slack = jnp.minimum(donor - 1, most - sink)
    shifted = jax.random.randint(jax.random.fold_in(rng, 1), (couples,), 0, 1 << 20) % (slack + 1)
    sizes = sizes.at[1:1 + 2 * couples:2].set(donor - shifted).at[2:2 + 2 * couples:2].set(sink + shifted)
    return sizes[jax.random.permutation(jax.random.fold_in(rng, 2), amount)]


def normal_values(rng, dims, deviation, limit, pieces=(), held_as=jnp.bfloat16):
    result = jax.random.normal(rng, dims, jnp.float32) * deviation
    if len(pieces) > 0:
        result = shard_levels(rng, dims, pieces, -0.22, 0.18) * result
    return jnp.clip(result, min=-limit, max=limit).astype(held_as)


def setup_inputs(seed: int = 0) -> dict:
    arg_keys = jax.random.split(jax.random.key(seed), 7)
    return {
        "acts": normal_values(arg_keys[0], (TOKENS, F), 2.0, 8.0, ((0, 8), (1, 32))),
        "sample_idx": place_ends(jax.random.randint(arg_keys[1], (N_ROW, CAP), 0, LOC), jax.random.fold_in(arg_keys[1], 1), 0, LOC - 1).astype(jnp.int32),
        "sample_count": uneven_parts(arg_keys[2], N_ROW, S, CAP, 2).astype(jnp.int32),
        "codes": draw_codes(jax.random.fold_in(arg_keys[6], 71), 0),
        "scales": jnp.clip(jnp.exp(math.log(0.00016) - 1.3862944 * jax.random.uniform(arg_keys[4], (F // QB, F), jnp.float32) ** shard_levels(arg_keys[4], (F // QB, F), ((0, 8), (1, 32)), -0.2, 0.2)), 3.9999998989515007e-05, 0.00016),
        "grad": normal_values(arg_keys[5], (F, M), 1.0, 6.0, ((0, 8), (1, 32))),
    }


ema_decay = 0.95
damping = 1.0

def pick_rows(local_tokens, positions):
    return jnp.take(local_tokens, positions, axis=0)

def reference(acts, sample_idx, sample_count, codes, scales, grad):
    local_tokens = acts.reshape(N_ROW, LOC, F)
    picked = jax.vmap(pick_rows)(local_tokens, sample_idx)
    slot_index = jnp.arange(CAP, dtype=jnp.int32)
    masked = jnp.where(slot_index[None, :, None] < sample_count[:, None, None], picked, jnp.zeros_like(picked))
    tokens = masked.reshape(N_ROW * CAP, F)
    block_count = F // P_SIZE

    def ema_block(block_index):
        start = block_index * P_SIZE
        block_cols = lax.dynamic_slice_in_dim(tokens, start, P_SIZE, 1)
        product = lax.dot_general(block_cols.astype(jnp.float32), tokens.astype(jnp.float32), (((0,), (0,)), ((), ())), preferred_element_type=jnp.float32)
        code_rows = lax.dynamic_slice_in_dim(codes, start, P_SIZE, 0).astype(jnp.float32)
        scale_rows = lax.dynamic_slice_in_dim(scales, block_index * (P_SIZE // QB), P_SIZE // QB, 0)
        old_ema = (code_rows.reshape(P_SIZE // QB, QB, F) * scale_rows[:, None, :]).reshape(P_SIZE, F)
        return (ema_decay * old_ema + (1.0 - ema_decay) / S * product).astype(jnp.bfloat16)
    new_ema = lax.map(ema_block, jnp.arange(block_count, dtype=jnp.int32)).reshape(F, F)
    panel_input = new_ema[:, :P_SIZE].astype(jnp.float32) + damping * jnp.eye(F, P_SIZE, dtype=jnp.float32)
    lead_factor = jnp.linalg.cholesky(panel_input[:P_SIZE])
    panel = lax.linalg.triangular_solve(lead_factor, panel_input, left_side=False, lower=True, transpose_a=True)
    leading = lax.linalg.triangular_solve(lead_factor, grad[:P_SIZE].astype(jnp.float32), left_side=True, lower=True)

    def step_block(block_index):
        start = block_index * P_SIZE
        glob_rows = start + jnp.arange(P_SIZE, dtype=jnp.int32)[:, None]
        glob_cols = jnp.arange(F, dtype=jnp.int32)[None, :]
        full_tile = lax.dynamic_slice_in_dim(new_ema, start, P_SIZE, 0).astype(jnp.float32) + damping * (glob_rows == glob_cols)
        panel_here = lax.dynamic_slice_in_dim(panel, start, P_SIZE, 0)
        trailing = full_tile - jnp.dot(panel_here, panel.T, precision=lax.Precision.HIGHEST)
        panel_wide = jnp.concatenate([panel_here, jnp.zeros((P_SIZE, F - P_SIZE), jnp.float32)], axis=1)
        lower_part = jnp.where(glob_rows >= glob_cols, panel_wide, 0.0)
        upper_part = jnp.where(glob_rows < P_SIZE, 0.0, trailing)
        return jnp.where(glob_cols < P_SIZE, lower_part, upper_part)
    factor_step = lax.map(step_block, jnp.arange(block_count, dtype=jnp.int32)).reshape(F, F)
    remainder = grad.astype(jnp.float32) - jnp.dot(panel, leading, precision=lax.Precision.HIGHEST)
    leading_wide = jnp.concatenate([leading, jnp.zeros((F - P_SIZE, M), jnp.float32)], axis=0)
    all_rows = jnp.arange(F, dtype=jnp.int32)[:, None]
    solved = jnp.where(all_rows < P_SIZE, leading_wide, remainder)
    return (new_ema, factor_step, solved)
```

```python
import jax
import jax.numpy as jnp
from jax import lax
from jax.sharding import PartitionSpec as P

PANEL = 256
SAMPLES = 256

ema_decay = 0.95
damping = 1.0
update_weight = (1.0 - ema_decay) / SAMPLES
bf16 = jnp.bfloat16
f32 = jnp.float32
HIGHEST = lax.Precision.HIGHEST


def gram(a, b):
    return lax.dot_general(a, b, (((0,), (0,)), ((), ())), preferred_element_type=f32)


def on_device(acts, sample_idx, sample_count, codes, scales, grad):
    rows_here, width = codes.shape
    grad_width = grad.shape[1]
    row_n = lax.axis_size("row")
    col_n = lax.axis_size("col")
    y_n = col_n // row_n
    z_n = col_n // y_n
    row = lax.axis_index("row")
    col = lax.axis_index("col")
    y = col % y_n
    y_groups = [[z * y_n + i for i in range(y_n)] for z in range(z_n)]
    z_groups = [[z * y_n + i for z in range(z_n)] for i in range(y_n)]
    swap = [
        (g * col_n + y_n * r + j, r * col_n + y_n * g + j)
        for g in range(row_n)
        for r in range(row_n)
        for j in range(y_n)
    ]
    part = SAMPLES // row_n
    quarter = rows_here // y_n
    piece = quarter // z_n
    capacity = sample_idx.shape[1]
    block = rows_here // scales.shape[0]

    with jax.named_scope("pick_samples"):
        before = jnp.sum(jnp.where(jnp.arange(row_n) < row, sample_count, 0))
        count_here = lax.dynamic_index_in_dim(sample_count, row, keepdims=False)
        slot = jnp.arange(capacity, dtype=jnp.int32)
        place = jnp.arange(SAMPLES, dtype=jnp.int32)
        takes = (place[:, None] - before == slot[None, :]) & (slot[None, :] < count_here)
        holds = sample_idx[0][:, None] == jnp.arange(acts.shape[0], dtype=jnp.int32)[None, :]
        choice = jnp.dot(takes.astype(bf16), holds.astype(bf16), preferred_element_type=f32)
        placed = jnp.dot(choice.astype(bf16), acts, preferred_element_type=f32).astype(bf16)
    with jax.named_scope("old_panel"):
        old_panel = (
            ema_decay
            * (
                codes[:, :PANEL].astype(f32).reshape(rows_here // block, block, PANEL)
                * scales[:, None, :PANEL]
            )
        ).reshape(rows_here, PANEL).astype(bf16)
    with jax.named_scope("row_scatter"):
        outgoing = jnp.concatenate([placed, grad[:SAMPLES], old_panel[:PANEL]], axis=1)
        incoming = lax.all_to_all(outgoing, "row", 0, 0, tiled=True).reshape(row_n, part, -1)
        own_slice = jnp.sum(incoming[:, :, :width].astype(f32), axis=0).astype(bf16)
        grad_slice = incoming[0, :, width : width + grad_width]
        lead_slice = incoming[0, :, width + grad_width :]
    with jax.named_scope("y_scatter"):
        old_quarter = old_panel[:quarter]
        slices = jnp.concatenate([own_slice[:, :PANEL], lead_slice], axis=0)
        for d in range(1, y_n):
            moved = lax.ppermute(old_panel[d * quarter : (d + 1) * quarter], "col", [(0, d)])
            old_quarter = jnp.where(y == d, moved, old_quarter)
        sent = slices
        for d in range(1, y_n):
            moved = lax.ppermute(sent, "col", [(0, d)])
            slices = jnp.where(y == d, moved, slices)
    with jax.named_scope("z_scatter"):
        outgoing = jnp.concatenate(
            [
                old_quarter.reshape(z_n, piece, PANEL),
                jnp.broadcast_to(slices[None], (z_n,) + slices.shape),
            ],
            axis=1,
        )
        incoming = lax.all_to_all(
            outgoing, "col", 0, 0, tiled=True, axis_index_groups=z_groups
        )[0]
        old_piece = incoming[:piece]
        slices = incoming[piece:]
    with jax.named_scope("swap_samples"):
        swapped = lax.ppermute(own_slice, ("row", "col"), swap)
    halves = width // PANEL
    with jax.named_scope("row_gather"):
        outgoing = jnp.concatenate(
            [slices, grad_slice]
            + [own_slice[:, h * PANEL : (h + 1) * PANEL] for h in range(halves)],
            axis=0,
        )
        incoming = lax.all_to_all(
            jnp.broadcast_to(outgoing[None], (row_n,) + outgoing.shape), "row", 0, 0, tiled=True
        )
        x_lead, old_lead, grad_lead, *x_cols = [
            incoming[:, i * part : (i + 1) * part].reshape(SAMPLES, PANEL) for i in range(3 + halves)
        ]
    with jax.named_scope("z_gather"):
        outgoing = jnp.concatenate(
            [old_piece] + [swapped[:, h * PANEL : (h + 1) * PANEL] for h in range(halves)], axis=0
        )
        incoming = lax.all_to_all(
            jnp.broadcast_to(outgoing[None], (z_n,) + outgoing.shape),
            "col",
            0,
            0,
            tiled=True,
            axis_index_groups=z_groups,
        )
        old_quarter = incoming[:, :piece].reshape(quarter, PANEL)
        x_quarter = [
            incoming[:, piece + h * part : piece + (h + 1) * part].reshape(SAMPLES, PANEL)
            for h in range(halves)
        ]
    with jax.named_scope("swap_panel"):
        old_cols = lax.ppermute(old_quarter, ("row", "col"), swap)
    with jax.named_scope("y_gather"):
        outgoing = jnp.concatenate([old_quarter] + x_quarter, axis=0)
        incoming = lax.all_to_all(
            jnp.broadcast_to(outgoing[None], (y_n,) + outgoing.shape),
            "col",
            0,
            0,
            tiled=True,
            axis_index_groups=y_groups,
        )
        old_rows = incoming[:, :quarter].reshape(rows_here, PANEL)
        x_rows = jnp.concatenate(
            [
                incoming[i, quarter + h * SAMPLES : quarter + (h + 1) * SAMPLES]
                for i in range(y_n)
                for h in range(halves)
            ],
            axis=1,
        )
    x_cols = jnp.concatenate(x_cols, axis=1)

    eye = jnp.eye(PANEL, dtype=f32)
    glob_rows = row * rows_here + jnp.arange(rows_here, dtype=jnp.int32)[:, None]
    glob_cols = col * width + jnp.arange(width, dtype=jnp.int32)[None, :]

    def panel_ema(x, old):
        return (old.astype(f32) + update_weight * gram(x, x_lead)).astype(bf16).astype(f32)

    with jax.named_scope("factor"):
        lead = panel_ema(x_lead, old_lead) + damping * eye
        lower = jnp.linalg.cholesky(lead)
        inverse = lax.linalg.triangular_solve(lower, eye, left_side=True, lower=True)
        leading = jnp.dot(inverse, grad_lead.astype(f32), precision=HIGHEST)
    with jax.named_scope("panel_cols"):
        cols_in = panel_ema(x_cols, old_cols) + damping * (
            glob_cols.T == jnp.arange(PANEL, dtype=jnp.int32)[None, :]
        )
        panel_cols = jnp.dot(cols_in, inverse.T, precision=HIGHEST)
    with jax.named_scope("panel_rows"):
        rows_in = panel_ema(x_rows, old_rows) + damping * (
            glob_rows == jnp.arange(PANEL, dtype=jnp.int32)[None, :]
        )
        panel = jnp.dot(rows_in, inverse.T, precision=HIGHEST)
    with jax.named_scope("new_average"):
        old_ema = (
            codes.astype(f32).reshape(rows_here // block, block, width) * scales[:, None, :]
        ).reshape(rows_here, width)
        new_ema = (ema_decay * old_ema + update_weight * gram(x_rows, x_cols)).astype(bf16)
    with jax.named_scope("trailing"):
        full_tile = new_ema.astype(f32) + damping * (glob_rows == glob_cols)
        trailing = full_tile - jnp.dot(panel, panel_cols.T, precision=HIGHEST)
        panel_here = jnp.concatenate(
            [panel, jnp.zeros((rows_here, width - PANEL), f32)], axis=1
        )
        lower_part = jnp.where(glob_rows >= glob_cols, panel_here, 0.0)
        upper_part = jnp.where(glob_rows < PANEL, 0.0, trailing)
        factor_step = jnp.where(glob_cols < PANEL, lower_part, upper_part)
    with jax.named_scope("solved_rows"):
        remainder = grad.astype(f32) - jnp.dot(panel, leading, precision=HIGHEST)
        leading_wide = jnp.concatenate(
            [leading, jnp.zeros((rows_here - PANEL, grad_width), f32)], axis=0
        )
        solved = jnp.where(glob_rows < PANEL, leading_wide, remainder)
    return (new_ema, factor_step, solved)


def solution(mesh):
    in_specs = (
        P("row", "col"),
        P("row", None),
        P(),
        P("row", "col"),
        P("row", "col"),
        P("row", "col"),
    )
    out_specs = (P("row", "col"), P("row", "col"), P("row", "col"))
    return jax.shard_map(
        on_device, mesh=mesh, in_specs=in_specs, out_specs=out_specs, check_vma=False
    )
```

```python
import functools
import jax
import jax.numpy as jnp
from jax import lax
from jax.experimental import pallas as pl
from jax.experimental.pallas import tpu as pltpu
from jax.sharding import PartitionSpec as P

PANEL = 256
SAMPLES = 256
STEP = 64

ema_decay = 0.95
damping = 1.0
update_weight = (1.0 - ema_decay) / SAMPLES
bf16 = jnp.bfloat16
f32 = jnp.float32


def shape(dims, dtype):
    return jax.ShapeDtypeStruct(dims, dtype)


def params(mib=24):
    return pltpu.CompilerParams(vmem_limit_bytes=mib << 20)


def cost(flops, moved):
    return pl.CostEstimate(flops=flops, bytes_accessed=moved, transcendentals=0)


def split(x):
    hi = x.astype(bf16)
    return hi, (x - hi.astype(f32)).astype(bf16)


def dot_nn(a, b):
    return lax.dot_general(a, b, (((1,), (0,)), ((), ())), preferred_element_type=f32)


def dot_nt(a, b):
    return lax.dot_general(a, b, (((1,), (1,)), ((), ())), preferred_element_type=f32)


def dot_tn(a, b):
    return lax.dot_general(a, b, (((0,), (0,)), ((), ())), preferred_element_type=f32)


def three(dot, a, b):
    return dot(a[0], b[0]) + (dot(a[0], b[1]) + dot(a[1], b[0]))


def row_ids(dims):
    return lax.broadcasted_iota(jnp.int32, dims, 0)


def col_ids(dims):
    return lax.broadcasted_iota(jnp.int32, dims, 1)


def old_panel_kernel(quarter, codes_ref, scales_ref, *out_refs):
    rows = codes_ref.shape[0]
    block = rows // scales_ref.shape[0]
    for i, start in enumerate(range(0, rows, block)):
        old = codes_ref[start : start + block, :].astype(f32) * scales_ref[i : i + 1, :]
        out_refs[start // quarter][start % quarter : start % quarter + block, :] = (
            ema_decay * old
        ).astype(bf16)


def old_panel(codes, scales, y_n):
    rows = codes.shape[0]
    quarter = rows // y_n
    return pl.pallas_call(
        functools.partial(old_panel_kernel, quarter),
        grid=(1,),
        in_specs=[
            pl.BlockSpec((rows, PANEL), lambda i: (0, 0)),
            pl.BlockSpec((scales.shape[0], PANEL), lambda i: (0, 0)),
        ],
        out_specs=[pl.BlockSpec((quarter, PANEL), lambda i: (0, 0))] * y_n,
        out_shape=[shape((quarter, PANEL), bf16)] * y_n,
        compiler_params=params(56),
        cost_estimate=cost(rows * PANEL * 2, rows * PANEL * 4),
        name="old_panel",
    )(codes, scales)


def pick_kernel(count_ref, acts_ref, idx_ref, grad_ref, lead_ref, out_ref):
    row = lax.axis_index("row")
    before = jnp.int32(0)
    here = jnp.int32(0)
    for g in range(count_ref.shape[0]):
        before = before + jnp.where(g < row, count_ref[g], 0)
        here = jnp.where(g == row, count_ref[g], here)
    tokens, width = acts_ref.shape
    capacity = idx_ref.shape[1]
    takes_dims = (SAMPLES, capacity)
    slot = col_ids(takes_dims)
    takes = (row_ids(takes_dims) - before == slot) & (slot < here)
    holds = row_ids((tokens, capacity)) == idx_ref[...]
    one = lambda mask: jnp.where(mask, 1.0, 0.0).astype(bf16)
    choice = dot_nt(one(takes), one(holds)).astype(bf16)
    out_ref[:, :width] = dot_nn(choice, acts_ref[...]).astype(bf16)
    out_ref[:, width : width + grad_ref.shape[1]] = grad_ref[...]
    out_ref[:, width + grad_ref.shape[1] :] = lead_ref[...]


def pick(counts, acts, idx, grad, lead):
    tokens, width = acts.shape
    grad_width = grad.shape[1]
    total = width + grad_width + PANEL
    return pl.pallas_call(
        pick_kernel,
        grid=(1,),
        in_specs=[
            pl.BlockSpec(memory_space=pltpu.SMEM),
            pl.BlockSpec(acts.shape, lambda i: (0, 0)),
            pl.BlockSpec(idx.shape, lambda i: (0, 0)),
            pl.BlockSpec((SAMPLES, grad_width), lambda i: (0, 0)),
            pl.BlockSpec((PANEL, PANEL), lambda i: (0, 0)),
        ],
        out_specs=pl.BlockSpec((SAMPLES, total), lambda i: (0, 0)),
        out_shape=shape((SAMPLES, total), bf16),
        compiler_params=params(),
        cost_estimate=cost(2 * SAMPLES * tokens * width, 3 * SAMPLES * total),
        name="pick",
    )(counts, acts, idx, grad, lead)


def eliminate(block):
    tiles = [block[8 * i : 8 * i + 8] for i in range(STEP // 8)]
    sub = row_ids((8, 2 * STEP))
    for j in range(0, STEP, 2):
        t, k = divmod(j, 8)
        c0 = [jnp.broadcast_to(x[:, j : j + 1], x.shape) for x in tiles[t:]]
        c1 = [jnp.broadcast_to(x[:, j + 1 : j + 2], x.shape) for x in tiles[t:]]
        r0, r1 = tiles[t][k : k + 1], tiles[t][k + 1 : k + 2]
        a, b, c = c0[0][k : k + 1], c0[0][k + 1 : k + 2], c1[0][k + 1 : k + 2]
        s0 = lax.rsqrt(a)
        low = b * s0
        u0 = r0 * s0
        s1 = lax.rsqrt(c - low * low)
        u1 = (r1 - low * u0) * s1
        for i in range(t, STEP // 8):
            v0 = c0[i - t] * s0
            v1 = (c1[i - t] - v0 * low) * s1
            new = tiles[i] - v0 * u0 - v1 * u1
            if i == t:
                kept = jnp.where(sub == k + 1, u1, tiles[i])
                new = jnp.where(sub > k + 1, new, jnp.where(sub == k, u0, kept))
            tiles[i] = new
    return jnp.concatenate(tiles, axis=0)


def factor_kernel(x_ref, old_ref, grad_ref, inv_hi_ref, inv_lo_ref, lead_ref, hi_ref, lo_ref, work):
    x = x_ref[...]
    lead = (old_ref[...].astype(f32) + update_weight * dot_tn(x, x)).astype(bf16).astype(f32)
    dims = (PANEL, PANEL)
    eye = jnp.where(row_ids(dims) == col_ids(dims), 1.0, 0.0)
    work[:, :PANEL] = 0.5 * (lead + lead.T) + damping * eye
    work[:, PANEL:] = eye
    small = jnp.where(row_ids((STEP, STEP)) == col_ids((STEP, STEP)), 1.0, 0.0)
    for start in range(0, PANEL, STEP):
        end = start + STEP
        done = eliminate(jnp.concatenate([work[start:end, start:end], small], axis=1))
        rows = three(dot_nn, split(done[:, STEP:]), split(work[start:end, :]))
        work[start:end, :] = rows
        if end < PANEL:
            hi, lo = split(rows)
            down = three(dot_tn, (hi[:, :PANEL], lo[:, :PANEL]), (hi, lo))
            work[end:, :] = work[end:, :] - down[end:, :]
    inv = split(jnp.where(row_ids(dims) >= col_ids(dims), work[:, PANEL:], 0.0))
    inv_hi_ref[...], inv_lo_ref[...] = inv
    leading = dot_nn(inv[0], grad_ref[...]) + dot_nn(inv[1], grad_ref[...])
    lead_ref[...] = leading
    hi_ref[...], lo_ref[...] = split(leading)


def factor(x_lead, old_lead, grad_lead):
    square = shape((PANEL, PANEL), bf16)
    return pl.pallas_call(
        factor_kernel,
        out_shape=(
            square,
            square,
            shape(grad_lead.shape, f32),
            shape(grad_lead.shape, bf16),
            shape(grad_lead.shape, bf16),
        ),
        scratch_shapes=[pltpu.VMEM((PANEL, 2 * PANEL), f32)],
        compiler_params=params(),
        cost_estimate=cost(16_000_000_000, PANEL * PANEL * 20),
        name="factor",
    )(x_lead, old_lead, grad_lead)


def panel_cols_kernel(x_ref, x_lead_ref, old_ref, inv_hi_ref, inv_lo_ref, hi_ref, lo_ref):
    inv = (inv_hi_ref[...], inv_lo_ref[...])
    product = dot_tn(x_ref[...], x_lead_ref[...])
    lead = (old_ref[...].astype(f32) + update_weight * product).astype(bf16).astype(f32)
    first = lax.axis_index("col") * old_ref.shape[0]
    diagonal = row_ids(lead.shape) + first == col_ids(lead.shape)
    lead = lead + jnp.where(diagonal, damping, 0.0)
    hi_ref[...], lo_ref[...] = split(three(dot_nt, split(lead), inv))


def panel_cols(x_cols, x_lead, old_cols, inv):
    out = shape(old_cols.shape, bf16)
    width = old_cols.shape[0]
    return pl.pallas_call(
        panel_cols_kernel,
        out_shape=(out, out),
        compiler_params=params(),
        cost_estimate=cost(8 * width * PANEL * PANEL, width * PANEL * 8),
        name="panel_cols",
    )(x_cols, x_lead, old_cols, *inv)


def rows_kernel(
    width,
    y_n,
    steps,
    quarter_ref,
    part_ref,
    codes_ref,
    scales_ref,
    grad_ref,
    x_cols_ref,
    x_lead_ref,
    inv_hi_ref,
    inv_lo_ref,
    cols_hi_ref,
    cols_lo_ref,
    lead_ref,
    lead_hi_ref,
    lead_lo_ref,
    *refs,
):
    ema_ref, step_ref, solved_ref = refs[-3:]
    half = pl.program_id(0)

    at = quarter_ref[0] * steps + half
    row = lax.axis_index("row")
    col = lax.axis_index("col")
    rows_here = y_n * steps * PANEL
    old = part_ref[pl.ds(pl.multiple_of(half * PANEL, PANEL), PANEL), :]
    x_at = pl.multiple_of((steps + half) * PANEL, PANEL)
    x = part_ref[pl.ds(x_at, SAMPLES), :]
    product = dot_tn(x, x_cols_ref[...])
    blocks = scales_ref.shape[0] // steps
    block = PANEL // blocks
    scale = scales_ref[:blocks, :]
    for i in range(1, steps):
        scale = jnp.where(half == i, scales_ref[i * blocks : (i + 1) * blocks, :], scale)
    pieces = []
    for i in range(blocks):
        piece = codes_ref[i * block : (i + 1) * block, :].astype(f32) * scale[i : i + 1, :]
        pieces.append(
            (
                ema_decay * piece + update_weight * product[i * block : (i + 1) * block, :]
            ).astype(bf16)
        )
    ema = jnp.concatenate(pieces, axis=0)
    ema_ref[...] = ema
    lead = (old.astype(f32) + update_weight * dot_tn(x, x_lead_ref[...])).astype(bf16)
    lead = lead.astype(f32)
    first_row = row * rows_here + at * PANEL
    is_first = first_row == 0
    square = (PANEL, PANEL)
    on_diagonal = (row_ids(square) + first_row) == col_ids(square)
    lead = lead + jnp.where(on_diagonal, damping, 0.0)
    panel = three(dot_nt, split(lead), (inv_hi_ref[...], inv_lo_ref[...]))
    pair = split(panel)
    wide = (PANEL, width)
    diagonal = (row_ids(wide) + first_row) == (col_ids(wide) + col * width)
    full = ema.astype(f32) + jnp.where(diagonal, damping, 0.0)
    step_ref[...] = full - three(dot_nt, pair, (cols_hi_ref[...], cols_lo_ref[...]))
    solved_ref[...] = grad_ref[...].astype(f32) - three(
        dot_nn, pair, (lead_hi_ref[...], lead_lo_ref[...])
    )

    @pl.when(is_first)
    def _():
        step_ref[...] = jnp.zeros(wide, f32)
        solved_ref[...] = lead_ref[...]

    @pl.when(col == 0)
    def _():
        lower = (row_ids(square) + first_row) >= col_ids(square)
        step_ref[:, :PANEL] = jnp.where(lower, panel, 0.0)


def rows(quarter_at, y_n, part, codes, scales, grad, held, before):
    rows_here, width = codes.shape
    grad_width = grad.shape[1]
    steps = rows_here // y_n // PANEL
    whole = lambda a: pl.BlockSpec(a.shape, lambda i, q: (0,) * a.ndim)
    block = lambda w: pl.BlockSpec((PANEL, w), lambda i, q: (q[0] * steps + i, 0))
    held = list(held)
    before = list(before)
    first = 5 + len(held)
    return pl.pallas_call(
        functools.partial(rows_kernel, width, y_n, steps),
        grid_spec=pltpu.PrefetchScalarGridSpec(
            num_scalar_prefetch=1,
            grid=(steps,),
            in_specs=[
                whole(part),
                block(width),
                pl.BlockSpec((scales.shape[0] // y_n, width), lambda i, q: (q[0], 0)),
                block(grad_width),
            ]
            + [whole(a) for a in held]
            + [pl.BlockSpec(memory_space=pl.ANY)] * len(before),
            out_specs=[block(width), block(width), block(grad_width)],
        ),
        out_shape=[
            shape((rows_here, width), bf16),
            shape((rows_here, width), f32),
            shape((rows_here, grad_width), f32),
        ],
        input_output_aliases={first + i: i for i in range(len(before))},
        compiler_params=params(),
        cost_estimate=cost(
            2 * steps * PANEL * PANEL * (width * 4 + PANEL * 7), steps * PANEL * width * 14
        ),
        name="rows",
    )(quarter_at, part, codes, scales, grad, *held, *before)


VMEM = pl.BlockSpec(memory_space=pltpu.VMEM)
ANYWHERE = pl.BlockSpec(memory_space=pl.ANY)


def shuffle(body, name, out_shapes, operands, ties=()):
    count = len(operands)

    def kernel(*refs):
        body(*refs[:count], *refs[count + len(ties) :])

    moved = sum(2 * o.size for o in operands)
    return pl.pallas_call(
        kernel,
        in_specs=[VMEM] * count + [ANYWHERE] * len(ties),
        out_shape=[shape(dims, bf16) for dims in out_shapes],
        compiler_params=params(),
        cost_estimate=cost(moved, 2 * moved),
        name=name,
    )(*operands, *ties)


def choose_y(y_n, own_ref, *refs):
    y = lax.rem(lax.axis_index("col"), y_n)
    value = own_ref[...]
    for d in range(1, y_n):
        value = jnp.where(y == d, refs[d - 1][...], value)
    return value


def old_quarter_kernel(y_n, *refs):
    refs[-1][...] = choose_y(y_n, *refs[:-1])


def unpack_kernel(row_n, width, grad_width, in_ref, own_ref, sent_ref, grad_ref):
    part = in_ref.shape[0] // row_n
    total = in_ref[:part, :width].astype(f32)
    for g in range(1, row_n):
        total = total + in_ref[g * part : (g + 1) * part, :width].astype(f32)
    own = total.astype(bf16)
    own_ref[...] = own
    sent_ref[:part, :] = own[:, :PANEL]
    sent_ref[part:, :] = in_ref[:part, width + grad_width :]
    grad_ref[...] = in_ref[:part, width : width + grad_width]


def row_pack_kernel(slices_ref, grad_ref, own_ref, out_ref):
    part = grad_ref.shape[0]
    for i in range(out_ref.shape[0]):
        out_ref[i, : 2 * part, :] = slices_ref[: 2 * part, :]
        out_ref[i, 2 * part : 3 * part, :] = grad_ref[...]
        for h in range(own_ref.shape[1] // PANEL):
            out_ref[i, (3 + h) * part : (4 + h) * part, :] = own_ref[:, h * PANEL : (h + 1) * PANEL]


def row_unpack_kernel(in_ref, x_lead_ref, old_lead_ref, grad_ref, cols_ref):
    part = SAMPLES // in_ref.shape[0]
    for i in range(in_ref.shape[0]):
        at = slice(i * part, (i + 1) * part)
        x_lead_ref[at, :] = in_ref[i, :part, :]
        old_lead_ref[at, :] = in_ref[i, part : 2 * part, :]
        grad_ref[at, :] = in_ref[i, 2 * part : 3 * part, :]
        for h in range(cols_ref.shape[1] // PANEL):
            cols_ref[at, h * PANEL : (h + 1) * PANEL] = in_ref[i, (3 + h) * part : (4 + h) * part, :]


def z_pack_kernel(y_n, piece, old_ref, x_ref, *refs):
    slices = choose_y(y_n, *refs[:-1])
    out_ref = refs[-1]
    part = x_ref.shape[0]
    halves = x_ref.shape[1] // PANEL
    for i in range(out_ref.shape[0]):
        out_ref[i, :piece, :] = old_ref[:piece, :]
        for h in range(halves):
            at = piece + h * part
            out_ref[i, at : at + part, :] = x_ref[:, h * PANEL : (h + 1) * PANEL]
        out_ref[i, piece + halves * part :, :] = slices


def z_unpack_kernel(piece, part, halves, in_ref, out_ref, old_ref, slices_ref):
    z_n = in_ref.shape[0]
    for i in range(z_n):
        out_ref[i * piece : (i + 1) * piece, :] = in_ref[i, :piece, :]
        old_ref[i * piece : (i + 1) * piece, :] = in_ref[i, :piece, :]
        for h in range(halves):
            at = z_n * piece + (h * z_n + i) * part
            out_ref[at : at + part, :] = in_ref[i, piece + h * part : piece + (h + 1) * part, :]
    slices_ref[...] = in_ref[0, piece + halves * part :, :]


def on_device(acts, sample_idx, sample_count, codes, scales, grad):
    rows_here, width = codes.shape
    grad_width = grad.shape[1]
    row_n = lax.axis_size("row")
    col_n = lax.axis_size("col")
    y_n = col_n // row_n
    z_n = col_n // y_n
    col = lax.axis_index("col")
    y = col % y_n
    z_groups = [[z * y_n + i for z in range(z_n)] for i in range(y_n)]
    swap = [
        (g * col_n + y_n * r + j, r * col_n + y_n * g + j)
        for g in range(row_n)
        for r in range(row_n)
        for j in range(y_n)
    ]

    def turn(d):
        return [(z * y_n + i, z * y_n + (i + d) % y_n) for z in range(z_n) for i in range(y_n)]

    part = SAMPLES // row_n
    quarter = rows_here // y_n
    piece = quarter // z_n
    halves = width // PANEL

    with jax.named_scope("old_panel"):
        old_quarters = old_panel(codes, scales, y_n)
    with jax.named_scope("old_to_y"):
        moved = [lax.ppermute(old_quarters[d], "col", [(0, d)]) for d in range(1, y_n)]
        (old_quarter,) = shuffle(
            functools.partial(old_quarter_kernel, y_n),
            "old_quarter",
            [(quarter, PANEL)],
            [old_quarters[0], *moved],
        )
    with jax.named_scope("row_scatter"):
        outgoing = pick(sample_count, acts, sample_idx, grad, old_quarters[0])
        incoming = lax.all_to_all(outgoing, "row", 0, 0, tiled=True)
        own_slice, sent, grad_slice = shuffle(
            functools.partial(unpack_kernel, row_n, width, grad_width),
            "unpack",
            [(part, width), (2 * part, PANEL), (part, grad_width)],
            [incoming],
            [old_quarter],
        )
    with jax.named_scope("old_to_z"):
        old_pieces = lax.all_to_all(
            old_quarter, "col", 0, 0, tiled=True, axis_index_groups=z_groups
        )
    with jax.named_scope("slices_to_y"):
        moved = [lax.ppermute(sent, "col", [(0, d)]) for d in range(1, y_n)]
    with jax.named_scope("swap_samples"):
        swapped = lax.ppermute(own_slice, ("row", "col"), swap)
    with jax.named_scope("z_gather"):
        (outgoing,) = shuffle(
            functools.partial(z_pack_kernel, y_n, piece),
            "z_pack",
            [(z_n, piece + (halves + 2) * part, PANEL)],
            [old_pieces, swapped, sent, *moved],
        )
        incoming = lax.all_to_all(outgoing, "col", 0, 0, tiled=True, axis_index_groups=z_groups)
        own_part, own_old, slices = shuffle(
            functools.partial(z_unpack_kernel, piece, part, halves),
            "z_unpack",
            [(quarter + halves * SAMPLES, PANEL), (quarter, PANEL), (2 * part, PANEL)],
            [incoming],
        )
    with jax.named_scope("row_gather"):
        (outgoing,) = shuffle(
            row_pack_kernel,
            "row_pack",
            [(row_n, (3 + halves) * part, PANEL)],
            [slices, grad_slice, own_slice],
        )
        incoming = lax.all_to_all(outgoing, "row", 0, 0, tiled=True)
        x_lead, old_lead, grad_lead, x_cols = shuffle(
            row_unpack_kernel,
            "row_unpack",
            [(SAMPLES, PANEL), (PANEL, PANEL), (PANEL, grad_width), (SAMPLES, width)],
            [incoming],
        )
    with jax.named_scope("parts_over_y"):
        parts = [own_part] + [lax.ppermute(own_part, "col", turn(d)) for d in (1, y_n - 1, y_n // 2)]
    with jax.named_scope("swap_panel"):
        old_cols = lax.ppermute(own_old, ("row", "col"), swap)
    with jax.named_scope("factor"):
        *inv, leading, lead_hi, lead_lo = factor(x_lead, old_lead, grad_lead)
    with jax.named_scope("panel_cols"):
        cols_pair = panel_cols(x_cols, x_lead, old_cols, inv)
    with jax.named_scope("rows"):
        held = (x_cols, x_lead, *inv, *cols_pair, leading, lead_hi, lead_lo)
        outs = ()
        for d, received in zip((0, 1, y_n - 1, y_n // 2), parts):
            at = lax.rem(y - d + y_n, y_n).astype(jnp.int32).reshape(1)
            outs = rows(at, y_n, received, codes, scales, grad, held, outs)
    return tuple(outs)


def solution(mesh):
    in_specs = (
        P("row", "col"),
        P("row", None),
        P(),
        P("row", "col"),
        P("row", "col"),
        P("row", "col"),
    )
    out_specs = (P("row", "col"), P("row", "col"), P("row", "col"))
    return jax.shard_map(
        on_device, mesh=mesh, in_specs=in_specs, out_specs=out_specs, check_vma=False
    )
```

```python
import functools
import jax
import jax.numpy as jnp
from jax import lax
from jax.experimental import pallas as pl
from jax.experimental.pallas import tpu as pltpu
from jax.sharding import PartitionSpec as P

PANEL = 256
SAMPLES = 256
STEP = 128

ema_decay = 0.95
damping = 1.0
update_weight = (1.0 - ema_decay) / SAMPLES
bf16 = jnp.bfloat16
f32 = jnp.float32


def shape(dims, dtype):
    return jax.ShapeDtypeStruct(dims, dtype)


def params(mib=24):
    return pltpu.CompilerParams(vmem_limit_bytes=mib << 20)


def cost(flops, moved):
    return pl.CostEstimate(flops=flops, bytes_accessed=moved, transcendentals=0)


def split(x):
    hi = x.astype(bf16)
    return hi, (x - hi.astype(f32)).astype(bf16)


def dot_nn(a, b):
    return lax.dot_general(a, b, (((1,), (0,)), ((), ())), preferred_element_type=f32)


def dot_nt(a, b):
    return lax.dot_general(a, b, (((1,), (1,)), ((), ())), preferred_element_type=f32)


def dot_tn(a, b):
    return lax.dot_general(a, b, (((0,), (0,)), ((), ())), preferred_element_type=f32)


def twice(x, axis):
    return jnp.concatenate([x, x], axis=axis)


def pair(x, axis):
    return jnp.concatenate(split(x), axis=axis)


def three(dot, a, b):
    return dot(a[0], b[0]) + (dot(a[0], b[1]) + dot(a[1], b[0]))


def row_ids(dims):
    return lax.broadcasted_iota(jnp.int32, dims, 0)


def col_ids(dims):
    return lax.broadcasted_iota(jnp.int32, dims, 1)


def old_panel_kernel(quarter, codes_ref, scales_ref, *out_refs):
    rows = codes_ref.shape[0]
    block = rows // scales_ref.shape[0]
    for i, start in enumerate(range(0, rows, block)):
        old = codes_ref[start : start + block, :].astype(f32) * scales_ref[i : i + 1, :]
        out_refs[start // quarter][start % quarter : start % quarter + block, :] = (
            ema_decay * old
        ).astype(bf16)


def old_panel(codes, scales, y_n):
    rows = codes.shape[0]
    quarter = rows // y_n
    return pl.pallas_call(
        functools.partial(old_panel_kernel, quarter),
        grid=(1,),
        in_specs=[
            pl.BlockSpec((rows, PANEL), lambda i: (0, 0)),
            pl.BlockSpec((scales.shape[0], PANEL), lambda i: (0, 0)),
        ],
        out_specs=[pl.BlockSpec((quarter, PANEL), lambda i: (0, 0))] * y_n,
        out_shape=[shape((quarter, PANEL), bf16)] * y_n,
        compiler_params=params(),
        cost_estimate=cost(rows * PANEL * 2, rows * PANEL * 4),
        name="old_panel",
    )(codes, scales)


def pick_kernel(block, count_ref, acts_ref, idx_ref, grad_ref, codes_ref, scales_ref, out_ref):
    row = lax.axis_index("row")
    before = jnp.int32(0)
    here = jnp.int32(0)
    for g in range(count_ref.shape[0]):
        before = before + jnp.where(g < row, count_ref[g], 0)
        here = jnp.where(g == row, count_ref[g], here)
    tokens, width = acts_ref.shape
    capacity = idx_ref.shape[1]
    takes_dims = (SAMPLES, capacity)
    slot = col_ids(takes_dims)
    takes = (row_ids(takes_dims) - before == slot) & (slot < here)
    holds = row_ids((tokens, capacity)) == idx_ref[...]
    one = lambda mask: jnp.where(mask, 1.0, 0.0).astype(bf16)
    choice = dot_nt(one(takes), one(holds)).astype(bf16)
    out_ref[:, :width] = dot_nn(choice, acts_ref[...]).astype(bf16)
    out_ref[:, width : width + grad_ref.shape[1]] = grad_ref[...]
    for i, start in enumerate(range(0, PANEL, block)):
        here = slice(start, start + block)
        old = ema_decay * (codes_ref[here, :].astype(f32) * scales_ref[i : i + 1, :])
        out_ref[here, width + grad_ref.shape[1] :] = old.astype(bf16)


def pick(counts, acts, idx, grad, codes, scales):
    tokens, width = acts.shape
    grad_width = grad.shape[1]
    total = width + grad_width + PANEL
    block = codes.shape[0] // scales.shape[0]
    return pl.pallas_call(
        functools.partial(pick_kernel, block),
        grid=(1,),
        in_specs=[
            pl.BlockSpec(memory_space=pltpu.SMEM),
            pl.BlockSpec(acts.shape, lambda i: (0, 0)),
            pl.BlockSpec(idx.shape, lambda i: (0, 0)),
            pl.BlockSpec((SAMPLES, grad_width), lambda i: (0, 0)),
            pl.BlockSpec((PANEL, PANEL), lambda i: (0, 0)),
            pl.BlockSpec((8, PANEL), lambda i: (0, 0)),
        ],
        out_specs=pl.BlockSpec((SAMPLES, total), lambda i: (0, 0)),
        out_shape=shape((SAMPLES, total), bf16),
        compiler_params=params(56),
        cost_estimate=cost(2 * SAMPLES * tokens * width, 3 * SAMPLES * total),
        name="pick",
    )(counts, acts, idx, grad, codes, scales)


def eliminate(block):
    tiles = [block[8 * i : 8 * i + 8] for i in range(STEP // 8)]
    sub = row_ids((8, 2 * STEP))
    for j in range(0, STEP, 2):
        t, k = divmod(j, 8)
        c0 = [jnp.broadcast_to(x[:, j : j + 1], x.shape) for x in tiles[t:]]
        c1 = [jnp.broadcast_to(x[:, j + 1 : j + 2], x.shape) for x in tiles[t:]]
        r0, r1 = tiles[t][k : k + 1], tiles[t][k + 1 : k + 2]
        a, b, c = c0[0][k : k + 1], c0[0][k + 1 : k + 2], c1[0][k + 1 : k + 2]
        s0 = lax.rsqrt(a)
        low = b * s0
        u0 = r0 * s0
        s1 = lax.rsqrt(c - low * low)
        u1 = (r1 - low * u0) * s1
        for i in range(t, STEP // 8):
            v0 = c0[i - t] * s0
            v1 = (c1[i - t] - v0 * low) * s1
            new = tiles[i] - v0 * u0 - v1 * u1
            if i == t:
                kept = jnp.where(sub == k + 1, u1, tiles[i])
                new = jnp.where(sub > k + 1, new, jnp.where(sub == k, u0, kept))
            tiles[i] = new
    return jnp.concatenate(tiles, axis=0)


def factor_kernel(x_ref, old_ref, grad_ref, inv_ref, inv_t_ref, lead_ref, lead_twice_ref, work):
    x = x_ref[:, x_ref.shape[1] - PANEL :]
    lead = (old_ref[...].astype(f32) + update_weight * dot_tn(x, x)).astype(bf16).astype(f32)
    dims = (PANEL, PANEL)
    eye = jnp.where(row_ids(dims) == col_ids(dims), 1.0, 0.0)
    work[:, :PANEL] = 0.5 * (lead + lead.T) + damping * eye
    work[:, PANEL:] = eye
    small = jnp.where(row_ids((STEP, STEP)) == col_ids((STEP, STEP)), 1.0, 0.0)
    for start in range(0, PANEL, STEP):
        end = start + STEP
        done = eliminate(jnp.concatenate([work[start:end, start:end], small], axis=1))
        rows = three(dot_nn, split(done[:, STEP:]), split(work[start:end, :]))
        work[start:end, :] = rows
        if end < PANEL:
            hi, lo = split(rows)
            down = three(dot_tn, (hi[:, :PANEL], lo[:, :PANEL]), (hi, lo))
            work[end:, :] = work[end:, :] - down[end:, :]
    inverse = jnp.where(row_ids(dims) >= col_ids(dims), work[:, PANEL:], 0.0)
    inv_ref[...] = pair(inverse, 1)
    inv_t_ref[...] = inverse.T
    inv = split(inverse)
    leading = dot_nn(inv[0], grad_ref[...]) + dot_nn(inv[1], grad_ref[...])
    lead_ref[...] = leading
    lead_twice_ref[...] = twice(leading.astype(bf16), 0)


def factor(x_all, old_lead, grad_lead):
    grad_width = grad_lead.shape[1]
    return pl.pallas_call(
        factor_kernel,
        out_shape=(
            shape((PANEL, 2 * PANEL), bf16),
            shape((PANEL, PANEL), f32),
            shape((PANEL, grad_width), f32),
            shape((2 * PANEL, grad_width), bf16),
        ),
        scratch_shapes=[pltpu.VMEM((PANEL, 2 * PANEL), f32)],
        compiler_params=params(),
        cost_estimate=cost(16_000_000_000, PANEL * PANEL * 20),
        name="factor",
    )(x_all, old_lead, grad_lead)


def panel_cols_kernel(x_ref, old_ref, inv_ref, inv_t_ref, out_ref):
    width = old_ref.shape[0]
    product = dot_tn(x_ref[:, :width], x_ref[:, width:])
    lead = (old_ref[...].astype(f32) + update_weight * product).astype(bf16)
    panel = dot_nt(twice(lead, 1), inv_ref[...])
    out_ref[...] = twice(panel.astype(bf16), 1)

    @pl.when(lax.axis_index("col") == 0)
    def _():
        first = panel[:PANEL] + damping * inv_t_ref[...]
        out_ref[:PANEL, :] = twice(first.astype(bf16), 1)


def panel_cols(x_all, old_cols, inv, inv_t):
    width = old_cols.shape[0]
    return pl.pallas_call(
        panel_cols_kernel,
        out_shape=shape((width, 2 * PANEL), bf16),
        compiler_params=params(),
        cost_estimate=cost(8 * width * PANEL * PANEL, width * PANEL * 8),
        name="panel_cols",
    )(x_all, old_cols, inv, inv_t)


def rows_kernel(
    width,
    part_n,
    halves,
    at_ref,
    codes_ref,
    scales_ref,
    grad_ref,
    x_all_ref,
    inv_ref,
    inv_t_ref,
    cols_ref,
    lead_ref,
    lead_twice_ref,
    *refs,
):
    part_refs = refs[:part_n]
    ema_ref, step_ref, solved_ref, part_ref = refs[part_n:]
    at = at_ref[pl.program_id(0)]
    row = lax.axis_index("row")
    col = lax.axis_index("col")
    count = halves * PANEL
    first_row = (row * part_n + at) * count
    for d in range(part_n):

        @pl.when(pl.program_id(0) == d)
        def _():
            part_ref[...] = part_refs[d][...]

    scale = ema_decay * scales_ref[...]
    blocks = scales_ref.shape[0] // halves
    block = PANEL // blocks
    for h in range(halves):
        rows_at = slice(h * PANEL, (h + 1) * PANEL)
        x = part_ref[count + h * SAMPLES : count + (h + 1) * SAMPLES, :]
        product = dot_tn(x, x_all_ref[...])
        lead = (part_ref[rows_at, :].astype(f32) + update_weight * product[:, width:]).astype(bf16)
        panel = dot_nt(twice(lead, 1), inv_ref[...])
        sides = pair(panel, 1)
        below = dot_nt(sides, cols_ref[...])
        for k in range(blocks):
            here = slice(k * block, (k + 1) * block)
            there = slice(h * PANEL + k * block, h * PANEL + (k + 1) * block)
            at_scale = h * blocks + k
            old_ema = codes_ref[there, :].astype(f32) * scale[at_scale : at_scale + 1, :]
            ema = (old_ema + update_weight * product[here, :width]).astype(bf16)
            ema_ref[there, :] = ema
            step_ref[there, :] = ema.astype(f32) - below[here, :]
        remainder = grad_ref[rows_at, :].astype(f32) - dot_nn(sides, lead_twice_ref[...])
        solved_ref[rows_at, :] = remainder

        @pl.when(col == 0)
        def _():
            step_ref[rows_at, :PANEL] = panel

    wide = (count, width)
    apart = first_row - col * width

    @pl.when((apart > -count) & (apart < width) & (col > 0))
    def _():
        diagonal = (row_ids(wide) + apart) == col_ids(wide)
        step_ref[...] += jnp.where(diagonal, damping, 0.0)

    @pl.when((apart > -count) & (apart < width) & (col == 0))
    def _():
        after = (count, width - PANEL)
        diagonal = (row_ids(after) + apart) == col_ids(after) + PANEL
        step_ref[:, PANEL:] += jnp.where(diagonal, damping, 0.0)

    @pl.when(first_row == 0)
    def _():
        square = (PANEL, PANEL)
        first = step_ref[:PANEL, :PANEL] + damping * inv_t_ref[...]
        kept = (row_ids(square) >= col_ids(square)) & (col == 0)
        step_ref[:PANEL, :PANEL] = jnp.where(kept, first, 0.0)
        step_ref[:PANEL, PANEL:] = jnp.zeros((PANEL, width - PANEL), f32)
        solved_ref[:PANEL, :] = lead_ref[...]


def rows(parts_at, parts, codes, scales, grad, held):
    rows_here, width = codes.shape
    grad_width = grad.shape[1]
    part_n = len(parts)
    count = rows_here // part_n
    whole = lambda a: pl.BlockSpec(a.shape, lambda i, q: (0,) * a.ndim)
    block = lambda h, w: pl.BlockSpec((h, w), lambda i, q: (q[i], 0))
    out_specs = [block(count, width), block(count, width), block(count, grad_width)]
    return pl.pallas_call(
        functools.partial(rows_kernel, width, part_n, count // PANEL),
        grid_spec=pltpu.PrefetchScalarGridSpec(
            num_scalar_prefetch=1,
            grid=(part_n,),
            in_specs=[
                block(count, width),
                block(scales.shape[0] // part_n, width),
                block(count, grad_width),
            ]
            + [whole(a) for a in (*held, *parts)],
            out_specs=out_specs,
            scratch_shapes=[pltpu.VMEM(parts[0].shape, bf16)],
        ),
        out_shape=[
            shape((rows_here, width), bf16),
            shape((rows_here, width), f32),
            shape((rows_here, grad_width), f32),
        ],
        compiler_params=params(),
        cost_estimate=cost(2 * rows_here * PANEL * (width * 3 + PANEL * 4), rows_here * width * 14),
        name="rows",
    )(parts_at, codes, scales, grad, *held, *parts)


VMEM = pl.BlockSpec(memory_space=pltpu.VMEM)
ANYWHERE = pl.BlockSpec(memory_space=pl.ANY)


def shuffle(body, name, out_shapes, operands, ties=(), room=0):
    count = len(operands)

    def kernel(*refs):
        body(*refs[:count], *refs[count + len(ties) :])

    moved = sum(2 * o.size for o in operands)
    return pl.pallas_call(
        kernel,
        in_specs=[VMEM] * count + [ANYWHERE] * len(ties),
        out_shape=[shape(dims, bf16) for dims in out_shapes],
        compiler_params=params(),
        cost_estimate=cost(moved + room, 2 * moved),
        name=name,
    )(*operands, *ties)


def choose_y(y_n, own_ref, *refs):
    y = lax.rem(lax.axis_index("col"), y_n)
    value = own_ref[...]
    for d in range(1, y_n):
        value = jnp.where(y == d, refs[d - 1][...], value)
    return value


def old_quarter_kernel(y_n, *refs):
    refs[-1][...] = choose_y(y_n, *refs[:-1])


def unpack_kernel(row_n, width, grad_width, in_ref, own_ref, sent_ref, grad_ref):
    part = in_ref.shape[0] // row_n
    total = in_ref[:part, :width].astype(f32)
    for g in range(1, row_n):
        total = total + in_ref[g * part : (g + 1) * part, :width].astype(f32)
    own = total.astype(bf16)
    own_ref[...] = own
    sent_ref[:part, :] = own[:, :PANEL]
    sent_ref[part:, :] = in_ref[:part, width + grad_width :]
    grad_ref[...] = in_ref[:part, width : width + grad_width]


def row_pack_kernel(slices_ref, old_ref, out_ref):
    rows = slices_ref.shape[0]
    for i in range(out_ref.shape[0]):
        out_ref[i, :rows, :] = slices_ref[...]
        out_ref[i, rows:, :] = old_ref[...]


def row_unpack_kernel(cols_in_ref, lead_in_ref, x_ref, old_lead_ref, grad_ref, old_ref):
    row_n = lead_in_ref.shape[0]
    part = SAMPLES // row_n
    each = cols_in_ref.shape[0] // row_n
    piece = old_ref.shape[0] // row_n
    halves = x_ref.shape[1] // PANEL - 1
    for i in range(row_n):
        at = slice(i * part, (i + 1) * part)
        x_ref[at, halves * PANEL :] = lead_in_ref[i, :part, :]
        old_lead_ref[at, :] = lead_in_ref[i, part : 2 * part, :]
        old_ref[i * piece : (i + 1) * piece, :] = lead_in_ref[i, 2 * part :, :]
        first = i * each
        grad_ref[at, :] = cols_in_ref[first : first + part, :]
        for h in range(halves):
            first = first + part
            x_ref[at, h * PANEL : (h + 1) * PANEL] = cols_in_ref[first : first + part, :]


def z_pack_kernel(y_n, piece, old_ref, x_ref, *refs):
    slices = choose_y(y_n, *refs[:-1])
    out_ref = refs[-1]
    part = x_ref.shape[0]
    halves = x_ref.shape[1] // PANEL
    for i in range(out_ref.shape[0]):
        out_ref[i, :piece, :] = old_ref[:piece, :]
        for h in range(halves):
            at = piece + h * part
            out_ref[i, at : at + part, :] = x_ref[:, h * PANEL : (h + 1) * PANEL]
        out_ref[i, piece + halves * part :, :] = slices


def cols_pack_kernel(grad_ref, own_ref, out_ref):
    part = grad_ref.shape[0]
    out_ref[:part, :] = grad_ref[...]
    for h in range(own_ref.shape[1] // PANEL):
        out_ref[(1 + h) * part : (2 + h) * part, :] = own_ref[:, h * PANEL : (h + 1) * PANEL]


def z_unpack_kernel(piece, part, halves, in_ref, out_ref, slices_ref):
    z_n = in_ref.shape[0]
    for i in range(z_n):
        out_ref[i * piece : (i + 1) * piece, :] = in_ref[i, :piece, :]
        for h in range(halves):
            at = z_n * piece + (h * z_n + i) * part
            out_ref[at : at + part, :] = in_ref[i, piece + h * part : piece + (h + 1) * part, :]
    slices_ref[...] = in_ref[0, piece + halves * part :, :]


def on_device(acts, sample_idx, sample_count, codes, scales, grad):
    rows_here, width = codes.shape
    grad_width = grad.shape[1]
    row_n = lax.axis_size("row")
    col_n = lax.axis_size("col")
    y_n = col_n // row_n
    z_n = col_n // y_n
    col = lax.axis_index("col")
    y = col % y_n
    z_groups = [[z * y_n + i for z in range(z_n)] for i in range(y_n)]
    swap = [
        (g * col_n + y_n * r + j, r * col_n + y_n * g + j)
        for g in range(row_n)
        for r in range(row_n)
        for j in range(y_n)
    ]

    def turn(d):
        return [(z * y_n + i, z * y_n + (i + d) % y_n) for z in range(z_n) for i in range(y_n)]

    part = SAMPLES // row_n
    quarter = rows_here // y_n
    piece = quarter // z_n
    halves = width // PANEL

    with jax.named_scope("old_panel"):
        old_quarters = old_panel(codes, scales, y_n)
    with jax.named_scope("old_to_y"):
        far_first = sorted(range(1, y_n), key=lambda d: -min(d, y_n - d))
        moved = {d: lax.ppermute(old_quarters[d], "col", [(0, d)]) for d in far_first}
        moved = [moved[d] for d in range(1, y_n)]
        (old_quarter,) = shuffle(
            functools.partial(old_quarter_kernel, y_n),
            "old_quarter",
            [(quarter, PANEL)],
            [old_quarters[0], *moved],
            room=0,
        )
    with jax.named_scope("row_scatter"):
        outgoing = pick(sample_count, acts, sample_idx, grad, codes, scales)
        incoming = lax.all_to_all(outgoing, "row", 0, 0, tiled=True)
        own_slice, sent, grad_slice = shuffle(
            functools.partial(unpack_kernel, row_n, width, grad_width),
            "unpack",
            [(part, width), (2 * part, PANEL), (part, grad_width)],
            [incoming],
            [old_quarter],
        )
    with jax.named_scope("old_to_z"):
        old_pieces = lax.all_to_all(
            old_quarter, "col", 0, 0, tiled=True, axis_index_groups=z_groups
        )
    with jax.named_scope("slices_to_y"):
        moved = [lax.ppermute(sent, "col", [(0, d)]) for d in range(1, y_n)]
    with jax.named_scope("swap_samples"):
        swapped = lax.ppermute(own_slice, ("row", "col"), swap)
    with jax.named_scope("z_gather"):
        (outgoing,) = shuffle(
            functools.partial(z_pack_kernel, y_n, piece),
            "z_pack",
            [(z_n, piece + (halves + 2) * part, PANEL)],
            [old_pieces, swapped, sent, *moved],
        )
        incoming = lax.all_to_all(outgoing, "col", 0, 0, tiled=True, axis_index_groups=z_groups)
        swapped_old = lax.ppermute(old_pieces[:piece], ("row", "col"), swap)
        (cols_block,) = shuffle(
            cols_pack_kernel,
            "cols_pack",
            [((1 + halves) * part, PANEL)],
            [grad_slice, own_slice],
            [outgoing],
        )
        cols_incoming = lax.all_gather(cols_block, "row", axis=0, tiled=True)
        own_part, slices = shuffle(
            functools.partial(z_unpack_kernel, piece, part, halves),
            "z_unpack",
            [(quarter + halves * SAMPLES, PANEL), (2 * part, PANEL)],
            [incoming],
            [cols_incoming, swapped_old],
        )
    with jax.named_scope("row_gather"):
        (lead_block,) = shuffle(
            row_pack_kernel, "row_pack", [(row_n, 2 * part + piece, PANEL)], [slices, swapped_old]
        )
        incoming = lax.all_to_all(lead_block, "row", 0, 0, tiled=True)
        x_all, old_lead, grad_lead, old_cols = shuffle(
            row_unpack_kernel,
            "row_unpack",
            [(SAMPLES, width + PANEL), (PANEL, PANEL), (PANEL, grad_width), (width, PANEL)],
            [cols_incoming, incoming],
        )
    with jax.named_scope("parts_over_y"):
        parts = [own_part] + [lax.ppermute(own_part, "col", turn(d)) for d in (1, y_n - 1, y_n // 2)]
    with jax.named_scope("factor"):
        inv, inv_t, leading, lead_twice = factor(x_all, old_lead, grad_lead)
    with jax.named_scope("panel_cols"):
        cols = panel_cols(x_all, old_cols, inv, inv_t)
    with jax.named_scope("rows"):
        shifts = jnp.array([0, 1, y_n - 1, y_n // 2], jnp.int32)
        parts_at = (y + y_n - shifts) % y_n
        held = (x_all, inv, inv_t, cols, leading, lead_twice)
        return tuple(rows(parts_at, parts, codes, scales, grad, held))


def solution(mesh):
    in_specs = (
        P("row", "col"),
        P("row", None),
        P(),
        P("row", "col"),
        P("row", "col"),
        P("row", "col"),
    )
    out_specs = (P("row", "col"), P("row", "col"), P("row", "col"))
    return jax.shard_map(
        on_device, mesh=mesh, in_specs=in_specs, out_specs=out_specs, check_vma=False
    )
```

```python
import functools
import jax
import jax.numpy as jnp
from jax import lax
from jax.experimental import pallas as pl
from jax.experimental.pallas import tpu as pltpu
from jax.sharding import PartitionSpec as P

PANEL = 256
SAMPLES = 256
STEP = 128

ema_decay = 0.95
damping = 1.0
update_weight = (1.0 - ema_decay) / SAMPLES
bf16 = jnp.bfloat16
f32 = jnp.float32


def shape(dims, dtype):
    return jax.ShapeDtypeStruct(dims, dtype)


def params(mib=24):
    return pltpu.CompilerParams(vmem_limit_bytes=mib << 20)


def cost(flops, moved):
    return pl.CostEstimate(flops=flops, bytes_accessed=moved, transcendentals=0)


def split(x):
    hi = x.astype(bf16)
    return hi, (x - hi.astype(f32)).astype(bf16)


def dot_nn(a, b):
    return lax.dot_general(a, b, (((1,), (0,)), ((), ())), preferred_element_type=f32)


def dot_nt(a, b):
    return lax.dot_general(a, b, (((1,), (1,)), ((), ())), preferred_element_type=f32)


def dot_tn(a, b):
    return lax.dot_general(a, b, (((0,), (0,)), ((), ())), preferred_element_type=f32)


def twice(x, axis):
    return jnp.concatenate([x, x], axis=axis)


def pair(x, axis):
    return jnp.concatenate(split(x), axis=axis)


def three(dot, a, b):
    return dot(a[0], b[0]) + (dot(a[0], b[1]) + dot(a[1], b[0]))


def row_ids(dims):
    return lax.broadcasted_iota(jnp.int32, dims, 0)


def col_ids(dims):
    return lax.broadcasted_iota(jnp.int32, dims, 1)


def old_panel_kernel(quarter, codes_ref, scales_ref, *out_refs):
    rows = codes_ref.shape[0]
    block = rows // scales_ref.shape[0]
    for i, start in enumerate(range(0, rows, block)):
        old = codes_ref[start : start + block, :].astype(f32) * scales_ref[i : i + 1, :]
        out_refs[start // quarter][start % quarter : start % quarter + block, :] = (
            ema_decay * old
        ).astype(bf16)


def old_panel(codes, scales, y_n):
    rows = codes.shape[0]
    quarter = rows // y_n
    return pl.pallas_call(
        functools.partial(old_panel_kernel, quarter),
        grid=(1,),
        in_specs=[
            pl.BlockSpec((rows, PANEL), lambda i: (0, 0)),
            pl.BlockSpec((scales.shape[0], PANEL), lambda i: (0, 0)),
        ],
        out_specs=[pl.BlockSpec((quarter, PANEL), lambda i: (0, 0))] * y_n,
        out_shape=[shape((quarter, PANEL), bf16)] * y_n,
        compiler_params=params(),
        cost_estimate=cost(rows * PANEL * 2, rows * PANEL * 4),
        name="old_panel",
    )(codes, scales)


def pick_kernel(block, count_ref, acts_ref, idx_ref, grad_ref, codes_ref, scales_ref, out_ref):
    row = lax.axis_index("row")
    before = jnp.int32(0)
    here = jnp.int32(0)
    for g in range(count_ref.shape[0]):
        before = before + jnp.where(g < row, count_ref[g], 0)
        here = jnp.where(g == row, count_ref[g], here)
    tokens, width = acts_ref.shape
    capacity = idx_ref.shape[1]
    takes_dims = (SAMPLES, capacity)
    slot = col_ids(takes_dims)
    takes = (row_ids(takes_dims) - before == slot) & (slot < here)
    holds = row_ids((tokens, capacity)) == idx_ref[...]
    one = lambda mask: jnp.where(mask, 1.0, 0.0).astype(bf16)
    choice = dot_nt(one(takes), one(holds)).astype(bf16)
    out_ref[:, :width] = dot_nn(choice, acts_ref[...]).astype(bf16)
    out_ref[:, width : width + grad_ref.shape[1]] = grad_ref[...]
    for i, start in enumerate(range(0, PANEL, block)):
        here = slice(start, start + block)
        old = ema_decay * (codes_ref[here, :].astype(f32) * scales_ref[i : i + 1, :])
        out_ref[here, width + grad_ref.shape[1] :] = old.astype(bf16)


def pick(counts, acts, idx, grad, codes, scales):
    tokens, width = acts.shape
    grad_width = grad.shape[1]
    total = width + grad_width + PANEL
    block = codes.shape[0] // scales.shape[0]
    return pl.pallas_call(
        functools.partial(pick_kernel, block),
        grid=(1,),
        in_specs=[
            pl.BlockSpec(memory_space=pltpu.SMEM),
            pl.BlockSpec(acts.shape, lambda i: (0, 0)),
            pl.BlockSpec(idx.shape, lambda i: (0, 0)),
            pl.BlockSpec((SAMPLES, grad_width), lambda i: (0, 0)),
            pl.BlockSpec((PANEL, PANEL), lambda i: (0, 0)),
            pl.BlockSpec((8, PANEL), lambda i: (0, 0)),
        ],
        out_specs=pl.BlockSpec((SAMPLES, total), lambda i: (0, 0)),
        out_shape=shape((SAMPLES, total), bf16),
        compiler_params=params(56),
        cost_estimate=cost(2 * SAMPLES * tokens * width, 3 * SAMPLES * total),
        name="pick",
    )(counts, acts, idx, grad, codes, scales)


def eliminate(block):
    tiles = [block[8 * i : 8 * i + 8] for i in range(STEP // 8)]
    sub = row_ids((8, 2 * STEP))
    for j in range(0, STEP, 2):
        t, k = divmod(j, 8)
        c0 = [jnp.broadcast_to(x[:, j : j + 1], x.shape) for x in tiles[t:]]
        c1 = [jnp.broadcast_to(x[:, j + 1 : j + 2], x.shape) for x in tiles[t:]]
        r0, r1 = tiles[t][k : k + 1], tiles[t][k + 1 : k + 2]
        a, b, c = c0[0][k : k + 1], c0[0][k + 1 : k + 2], c1[0][k + 1 : k + 2]
        s0 = lax.rsqrt(a)
        low = b * s0
        u0 = r0 * s0
        s1 = lax.rsqrt(c - low * low)
        u1 = (r1 - low * u0) * s1
        for i in range(t, STEP // 8):
            v0 = c0[i - t] * s0
            v1 = (c1[i - t] - v0 * low) * s1
            new = tiles[i] - v0 * u0 - v1 * u1
            if i == t:
                kept = jnp.where(sub == k + 1, u1, tiles[i])
                new = jnp.where(sub > k + 1, new, jnp.where(sub == k, u0, kept))
            tiles[i] = new
    return jnp.concatenate(tiles, axis=0)


def factor_kernel(x_ref, old_ref, grad_ref, inv_ref, inv_t_ref, lead_ref, lead_twice_ref, work):
    x = x_ref[:, x_ref.shape[1] - PANEL :]
    lead = (old_ref[...].astype(f32) + update_weight * dot_tn(x, x)).astype(bf16).astype(f32)
    dims = (PANEL, PANEL)
    eye = jnp.where(row_ids(dims) == col_ids(dims), 1.0, 0.0)
    work[:, :PANEL] = 0.5 * (lead + lead.T) + damping * eye
    work[:, PANEL:] = eye
    small = jnp.where(row_ids((STEP, STEP)) == col_ids((STEP, STEP)), 1.0, 0.0)
    for start in range(0, PANEL, STEP):
        end = start + STEP
        done = eliminate(jnp.concatenate([work[start:end, start:end], small], axis=1))
        rows = three(dot_nn, split(done[:, STEP:]), split(work[start:end, :]))
        work[start:end, :] = rows
        if end < PANEL:
            hi, lo = split(rows)
            down = three(dot_tn, (hi[:, :PANEL], lo[:, :PANEL]), (hi, lo))
            work[end:, :] = work[end:, :] - down[end:, :]
    inverse = jnp.where(row_ids(dims) >= col_ids(dims), work[:, PANEL:], 0.0)
    inverse_t = inverse.T
    inv_ref[...] = pair(inverse_t, 0)
    inv_t_ref[...] = inverse_t
    inv = split(inverse)
    leading = dot_nn(inv[0], grad_ref[...]) + dot_nn(inv[1], grad_ref[...])
    lead_ref[...] = leading
    lead_twice_ref[...] = twice(leading.astype(bf16), 0)


def factor(x_all, old_lead, grad_lead):
    grad_width = grad_lead.shape[1]
    return pl.pallas_call(
        factor_kernel,
        out_shape=(
            shape((2 * PANEL, PANEL), bf16),
            shape((PANEL, PANEL), f32),
            shape((PANEL, grad_width), f32),
            shape((2 * PANEL, grad_width), bf16),
        ),
        scratch_shapes=[pltpu.VMEM((PANEL, 2 * PANEL), f32)],
        compiler_params=params(),
        cost_estimate=cost(16_000_000_000, PANEL * PANEL * 20),
        name="factor",
    )(x_all, old_lead, grad_lead)


def panel_cols_kernel(x_ref, old_ref, inv_ref, inv_t_ref, lead_ref, out_ref):
    width = old_ref.shape[0]
    product = dot_tn(x_ref[:, :width], x_ref[:, width:])
    lead = (old_ref[...].astype(f32) + update_weight * product).astype(bf16)
    panel = dot_nn(twice(lead, 1), inv_ref[...])
    out_ref[:, :width] = twice(panel.T.astype(bf16), 0)
    out_ref[:, width:] = lead_ref[...]

    @pl.when(lax.axis_index("col") == 0)
    def _():
        first = panel[:PANEL] + damping * inv_t_ref[...]
        out_ref[:, :PANEL] = twice(first.T.astype(bf16), 0)


def panel_cols(x_all, old_cols, inv, inv_t, lead_twice):
    width = old_cols.shape[0]
    return pl.pallas_call(
        panel_cols_kernel,
        out_shape=shape((2 * PANEL, width + lead_twice.shape[1]), bf16),
        compiler_params=params(),
        cost_estimate=cost(8 * width * PANEL * PANEL, width * PANEL * 8),
        name="panel_cols",
    )(x_all, old_cols, inv, inv_t, lead_twice)


def rows_kernel(
    width,
    y_n,
    part_n,
    halves,
    at_ref,
    codes_ref,
    scales_ref,
    grad_ref,
    x_all_ref,
    inv_ref,
    inv_t_ref,
    weights_ref,
    lead_ref,
    *refs,
):
    part_refs = refs[:part_n]
    ema_ref, step_ref, solved_ref, part_ref = refs[-4:]
    at = at_ref[pl.program_id(0)]
    row = lax.axis_index("row")
    col = lax.axis_index("col")
    count = halves * PANEL
    first_row = (row * y_n + at) * count
    for d in range(part_n):

        @pl.when(pl.program_id(0) == d)
        def _():
            part_ref[...] = part_refs[d][...]

    scale = ema_decay * scales_ref[...]
    blocks = scales_ref.shape[0] // halves
    block = PANEL // blocks
    for h in range(halves):
        rows_at = slice(h * PANEL, (h + 1) * PANEL)
        x = part_ref[count + h * SAMPLES : count + (h + 1) * SAMPLES, :]
        product = dot_nn(x, x_all_ref[...])
        lead = (part_ref[rows_at, :].astype(f32) + update_weight * product[:, width:]).astype(bf16)
        panel = dot_nn(twice(lead, 1), inv_ref[...])
        below = dot_nn(pair(panel, 1), weights_ref[...])
        for k in range(blocks):
            here = slice(k * block, (k + 1) * block)
            there = slice(h * PANEL + k * block, h * PANEL + (k + 1) * block)
            at_scale = h * blocks + k
            old_ema = codes_ref[there, :].astype(f32) * scale[at_scale : at_scale + 1, :]
            ema = (old_ema + update_weight * product[here, :width]).astype(bf16)
            ema_ref[there, :] = ema
            step_ref[there, :] = ema.astype(f32) - below[here, :width]
        solved_ref[rows_at, :] = grad_ref[rows_at, :].astype(f32) - below[:, width:]

        @pl.when(col == 0)
        def _():
            step_ref[rows_at, :PANEL] = panel

    wide = (count, width)
    apart = first_row - col * width

    @pl.when((apart > -count) & (apart < width) & (col > 0))
    def _():
        diagonal = (row_ids(wide) + apart) == col_ids(wide)
        step_ref[...] += jnp.where(diagonal, damping, 0.0)

    @pl.when((apart > -count) & (apart < width) & (col == 0))
    def _():
        after = (count, width - PANEL)
        diagonal = (row_ids(after) + apart) == col_ids(after) + PANEL
        step_ref[:, PANEL:] += jnp.where(diagonal, damping, 0.0)

    @pl.when(first_row == 0)
    def _():
        square = (PANEL, PANEL)
        first = step_ref[:PANEL, :PANEL] + damping * inv_t_ref[...]
        kept = (row_ids(square) >= col_ids(square)) & (col == 0)
        step_ref[:PANEL, :PANEL] = jnp.where(kept, first, 0.0)
        step_ref[:PANEL, PANEL:] = jnp.zeros((PANEL, width - PANEL), f32)
        solved_ref[:PANEL, :] = lead_ref[...]


def rows(parts_at, y_n, parts, codes, scales, grad, held, before):
    rows_here, width = codes.shape
    grad_width = grad.shape[1]
    part_n = len(parts)
    count = rows_here // y_n
    first = 4 + len(held) + part_n
    whole = lambda a: pl.BlockSpec(a.shape, lambda i, q: (0,) * a.ndim)
    block = lambda h, w: pl.BlockSpec((h, w), lambda i, q: (q[i], 0))
    out_specs = [block(count, width), block(count, width), block(count, grad_width)]
    return pl.pallas_call(
        functools.partial(rows_kernel, width, y_n, part_n, count // PANEL),
        grid_spec=pltpu.PrefetchScalarGridSpec(
            num_scalar_prefetch=1,
            grid=(part_n,),
            in_specs=[
                block(count, width),
                block(scales.shape[0] // y_n, width),
                block(count, grad_width),
            ]
            + [whole(a) for a in (*held, *parts)]
            + [pl.BlockSpec(memory_space=pl.ANY)] * len(before),
            out_specs=out_specs,
            scratch_shapes=[pltpu.VMEM(parts[0].shape, bf16)],
        ),
        out_shape=[
            shape((rows_here, width), bf16),
            shape((rows_here, width), f32),
            shape((rows_here, grad_width), f32),
        ],
        input_output_aliases={first + i: i for i in range(len(before))},
        compiler_params=params(),
        cost_estimate=cost(
            2 * part_n * count * PANEL * (width * 3 + PANEL * 4), part_n * count * width * 14
        ),
        name="rows",
    )(parts_at, codes, scales, grad, *held, *parts, *before)


VMEM = pl.BlockSpec(memory_space=pltpu.VMEM)
ANYWHERE = pl.BlockSpec(memory_space=pl.ANY)


def shuffle(body, name, out_shapes, operands, ties=(), room=0):
    count = len(operands)

    def kernel(*refs):
        body(*refs[:count], *refs[count + len(ties) :])

    moved = sum(2 * o.size for o in operands)
    return pl.pallas_call(
        kernel,
        in_specs=[VMEM] * count + [ANYWHERE] * len(ties),
        out_shape=[shape(dims, bf16) for dims in out_shapes],
        compiler_params=params(),
        cost_estimate=cost(moved + room, 2 * moved),
        name=name,
    )(*operands, *ties)


def choose_y(y_n, own_ref, *refs):
    y = lax.rem(lax.axis_index("col"), y_n)
    value = own_ref[...]
    for d in range(1, y_n):
        value = jnp.where(y == d, refs[d - 1][...], value)
    return value


def old_quarter_kernel(y_n, *refs):
    refs[-1][...] = choose_y(y_n, *refs[:-1])


def unpack_kernel(row_n, width, grad_width, in_ref, own_ref, sent_ref, grad_ref):
    part = in_ref.shape[0] // row_n
    total = in_ref[:part, :width].astype(f32)
    for g in range(1, row_n):
        total = total + in_ref[g * part : (g + 1) * part, :width].astype(f32)
    own = total.astype(bf16)
    own_ref[...] = own
    sent_ref[:part, :] = own[:, :PANEL]
    sent_ref[part:, :] = in_ref[:part, width + grad_width :]
    grad_ref[...] = in_ref[:part, width : width + grad_width]


def row_pack_kernel(slices_ref, old_ref, out_ref):
    rows = slices_ref.shape[0]
    for i in range(out_ref.shape[0]):
        out_ref[i, :rows, :] = slices_ref[...]
        out_ref[i, rows:, :] = old_ref[...]


def row_unpack_kernel(cols_in_ref, lead_in_ref, x_ref, old_lead_ref, grad_ref, old_ref):
    row_n = lead_in_ref.shape[0]
    part = SAMPLES // row_n
    each = cols_in_ref.shape[0] // row_n
    piece = old_ref.shape[0] // row_n
    halves = x_ref.shape[1] // PANEL - 1
    for i in range(row_n):
        at = slice(i * part, (i + 1) * part)
        x_ref[at, halves * PANEL :] = lead_in_ref[i, :part, :]
        old_lead_ref[at, :] = lead_in_ref[i, part : 2 * part, :]
        old_ref[i * piece : (i + 1) * piece, :] = lead_in_ref[i, 2 * part :, :]
        first = i * each
        grad_ref[at, :] = cols_in_ref[first : first + part, :]
        for h in range(halves):
            first = first + part
            x_ref[at, h * PANEL : (h + 1) * PANEL] = cols_in_ref[first : first + part, :]


def z_pack_kernel(y_n, piece, old_ref, x_ref, *refs):
    slices = choose_y(y_n, *refs[:-1])
    out_ref = refs[-1]
    part = x_ref.shape[0]
    halves = x_ref.shape[1] // PANEL
    for i in range(out_ref.shape[0]):
        out_ref[i, :piece, :] = old_ref[:piece, :]
        for h in range(halves):
            at = piece + h * part
            out_ref[i, at : at + part, :] = x_ref[:, h * PANEL : (h + 1) * PANEL]
        out_ref[i, piece + halves * part :, :] = slices


def cols_pack_kernel(grad_ref, own_ref, out_ref):
    part = grad_ref.shape[0]
    out_ref[:part, :] = grad_ref[...]
    for h in range(own_ref.shape[1] // PANEL):
        out_ref[(1 + h) * part : (2 + h) * part, :] = own_ref[:, h * PANEL : (h + 1) * PANEL]


def z_unpack_kernel(piece, part, halves, in_ref, out_ref, slices_ref):
    z_n = in_ref.shape[0]
    for i in range(z_n):
        out_ref[i * piece : (i + 1) * piece, :] = in_ref[i, :piece, :]
    for h in range(halves):
        x_at = slice(piece + h * part, piece + (h + 1) * part)
        x = jnp.concatenate([in_ref[i, x_at, :] for i in range(z_n)], axis=0)
        at = z_n * piece + h * PANEL
        out_ref[at : at + PANEL, :] = x.T
    slices_ref[...] = in_ref[0, piece + halves * part :, :]


def on_device(acts, sample_idx, sample_count, codes, scales, grad):
    rows_here, width = codes.shape
    grad_width = grad.shape[1]
    row_n = lax.axis_size("row")
    col_n = lax.axis_size("col")
    y_n = col_n // row_n
    z_n = col_n // y_n
    col = lax.axis_index("col")
    y = col % y_n
    z_groups = [[z * y_n + i for z in range(z_n)] for i in range(y_n)]
    swap = [
        (g * col_n + y_n * r + j, r * col_n + y_n * g + j)
        for g in range(row_n)
        for r in range(row_n)
        for j in range(y_n)
    ]

    def turn(d):
        return [(z * y_n + i, z * y_n + (i + d) % y_n) for z in range(z_n) for i in range(y_n)]

    part = SAMPLES // row_n
    quarter = rows_here // y_n
    piece = quarter // z_n
    halves = width // PANEL

    with jax.named_scope("old_panel"):
        old_quarters = old_panel(codes, scales, y_n)
    with jax.named_scope("old_to_y"):
        far_first = sorted(range(1, y_n), key=lambda d: -min(d, y_n - d))
        moved = {d: lax.ppermute(old_quarters[d], "col", [(0, d)]) for d in far_first}
        moved = [moved[d] for d in range(1, y_n)]
        (old_quarter,) = shuffle(
            functools.partial(old_quarter_kernel, y_n),
            "old_quarter",
            [(quarter, PANEL)],
            [old_quarters[0], *moved],
            room=0,
        )
    with jax.named_scope("row_scatter"):
        outgoing = pick(sample_count, acts, sample_idx, grad, codes, scales)
        incoming = lax.all_to_all(outgoing, "row", 0, 0, tiled=True)
        own_slice, sent, grad_slice = shuffle(
            functools.partial(unpack_kernel, row_n, width, grad_width),
            "unpack",
            [(part, width), (2 * part, PANEL), (part, grad_width)],
            [incoming],
            [old_quarter],
        )
    with jax.named_scope("old_to_z"):
        old_pieces = lax.all_to_all(
            old_quarter, "col", 0, 0, tiled=True, axis_index_groups=z_groups
        )
    with jax.named_scope("slices_to_y"):
        moved = [lax.ppermute(sent, "col", [(0, d)]) for d in range(1, y_n)]
    with jax.named_scope("swap_samples"):
        swapped = lax.ppermute(own_slice, ("row", "col"), swap)
    with jax.named_scope("z_gather"):
        (outgoing,) = shuffle(
            functools.partial(z_pack_kernel, y_n, piece),
            "z_pack",
            [(z_n, piece + (halves + 2) * part, PANEL)],
            [old_pieces, swapped, sent, *moved],
        )
        incoming = lax.all_to_all(outgoing, "col", 0, 0, tiled=True, axis_index_groups=z_groups)
        swapped_old = lax.ppermute(old_pieces[:piece], ("row", "col"), swap)
        (cols_block,) = shuffle(
            cols_pack_kernel,
            "cols_pack",
            [((1 + halves) * part, PANEL)],
            [grad_slice, own_slice],
            [outgoing],
        )
        cols_incoming = lax.all_gather(cols_block, "row", axis=0, tiled=True)
        own_part, slices = shuffle(
            functools.partial(z_unpack_kernel, piece, part, halves),
            "z_unpack",
            [(quarter + halves * PANEL, PANEL), (2 * part, PANEL)],
            [incoming],
            [cols_incoming, swapped_old],
        )
    with jax.named_scope("row_gather"):
        (lead_block,) = shuffle(
            row_pack_kernel, "row_pack", [(row_n, 2 * part + piece, PANEL)], [slices, swapped_old]
        )
        incoming = lax.all_to_all(lead_block, "row", 0, 0, tiled=True)
        x_all, old_lead, grad_lead, old_cols = shuffle(
            row_unpack_kernel,
            "row_unpack",
            [(SAMPLES, width + PANEL), (PANEL, PANEL), (PANEL, grad_width), (width, PANEL)],
            [cols_incoming, incoming],
        )
    with jax.named_scope("parts_over_y"):
        parts = [own_part] + [lax.ppermute(own_part, "col", turn(d)) for d in (1, y_n - 1, y_n // 2)]
    with jax.named_scope("factor"):
        inv, inv_t, leading, lead_twice = factor(x_all, old_lead, grad_lead)
    with jax.named_scope("panel_cols"):
        weights = panel_cols(x_all, old_cols, inv, inv_t, lead_twice)
    with jax.named_scope("rows"):
        shifts = jnp.array([0, 1, y_n - 1, y_n // 2], jnp.int32)
        parts_at = (y + y_n - shifts) % y_n
        held = (x_all, inv, inv_t, weights, leading)
        outs = rows(parts_at[:1], y_n, parts[:1], codes, scales, grad, held, ())
        outs = rows(parts_at[1:], y_n, parts[1:], codes, scales, grad, held, outs)
        return tuple(outs)


def solution(mesh):
    in_specs = (
        P("row", "col"),
        P("row", None),
        P(),
        P("row", "col"),
        P("row", "col"),
        P("row", "col"),
    )
    out_specs = (P("row", "col"), P("row", "col"), P("row", "col"))
    return jax.shard_map(
        on_device, mesh=mesh, in_specs=in_specs, out_specs=out_specs, check_vma=False
    )
```
